32 devices in a mesh: ctx: 4 (over y, x), exp: 8 (over z, core).
Axes of the slice: x: 2, y: 2, z: 4, core: 2. Of those that a mesh axis runs over, the one named last changes fastest.
Arguments:
- query: bfloat16 [8, 256, 2048], P('exp', 'ctx'), may hold values from -24 to 24
- key_value: bfloat16 [8, 256, 2, 256], P('exp', 'ctx'), may hold values from -24 to 24
- positions: int32 [8, 256], P('exp', 'ctx'), may hold values from 0 to 255, as said below
- resid: bfloat16 [8, 256, 1440], P('exp', 'ctx'), may hold values from -6 to 6
- sinks: float32 [32], replicated, may hold values from -2 to 3
- o_weight: bfloat16 [2048, 1440], P('exp'), may hold values from -0.125 to 0.125
- norm_gain: float32 [1440], replicated, may hold values from 0.25 to 1.75
- expert_ids: int32 [8, 256, 4], P('exp', 'ctx'), may hold values from 0 to 7, all different within a row; in each aligned block of 64 rows (0 to 63, 64 to 127, ..., all dimensions but the last counted through in order) at most 32 rows name the same one
- route_weights: float32 [8, 256, 4], P('exp', 'ctx'), may hold values from 0.1 to 0.5
- w_gate: bfloat16 [1440, 11520], P(None, ('ctx', 'exp')), may hold values from -0.15625 to 0.15625
- w_up: bfloat16 [1440, 11520], P(None, ('ctx', 'exp')), may hold values from -0.15625 to 0.15625
- w_down: bfloat16 [11520, 1440], P(('ctx', 'exp')), may hold values from -0.15625 to 0.15625
Outputs:
- out: bfloat16 [8, 256, 1440], P('exp', 'ctx')
The draws below stay inside these ranges and needn't reach their ends.
Inputs may be any that keep to these rules, and one draw needn't show every extreme that they name: Within each sequence every position appears once; the 64 stored rows of one device are two runs of 32 consecutive ascending positions, each run starting at a multiple of 32. `expert_ids`: each row names 4 different experts; among the 64 rows of one device no expert is named more than 32 times, a bound that some block reaches.
All inputs are finite; a program needn't handle non-finite values.
Results may differ from the reference program's by a relative error of at most 0.0075.
Values may be sent and summed in bfloat16 or wider, within the bound.
A program may use at most 64 MiB of HBM per device.

```python
import math
import jax
import jax.numpy as jnp
import numpy as np
from jax import lax

D = 1440
QH = 32
KVH = 4
HD = 64
FF_E = 1440
TOP = 4
SLICES = 4
TOK_DEV = 64
SEQS = 8
LENGTH = 256
HALF = 32
EXPERTS = 8
CAP = 32
N_CTX = 4
N_EXP = 8


def draw_query(key, part):
    shape = (SEQS, LENGTH, QH * HD)
    noise = jnp.clip(jax.random.normal(jax.random.fold_in(key, 1), shape, jnp.float32), -6.0, 6.0)
    return noise.astype(jnp.bfloat16)


def draw_key_value(key, part):
    shape = (SEQS, LENGTH, 2, KVH * HD)
    values = jnp.clip(jax.random.normal(jax.random.fold_in(key, 2), shape, jnp.float32), -6.0, 6.0)
    return values.astype(jnp.bfloat16)


def draw_positions(key, part):
    blocks = LENGTH // HALF
    keys = jax.random.split(jax.random.fold_in(key, 3), SEQS)
    order = jax.vmap(lambda single: jax.random.permutation(single, blocks))(keys)
    spread = order[:, :, None] * HALF + jnp.arange(HALF)[None, None, :]
    return spread.reshape(SEQS, LENGTH).astype(jnp.int32)


def shard_levels(stream_key, extent, cuts, low, largest):
    factor_of, own = 1.0, jax.random.fold_in(stream_key, 6)
    for position, blocks in cuts:
        heights = jnp.exp(jax.random.uniform(jax.random.fold_in(own, position), (blocks,), jnp.float32, low / len(cuts), largest / len(cuts)))
        factor_of = factor_of * jnp.repeat(heights, extent[position] // blocks).reshape([-1 if axis == position else 1 for axis in range(len(extent))])
    return factor_of


def deal_out(stream_key, own, number, rows, amount, top, most, lean):
    sequence = jax.random.permutation(stream_key, amount)
    crowded, common = portions_of(amount, rows * top, most, lean, True), portions_of(amount, rows * top, most, lean, False)
    places = jnp.arange(amount)

    def named(lengths, turn):
        used = int((lengths > 0).sum())
        fixed = max(1, used // 4)
        passed = fixed + (places - fixed + turn * (used - fixed)) % max(1, amount - fixed)
        return jnp.zeros((amount,), jnp.int32).at[sequence[jnp.where(places < fixed, places, passed)]].set(jnp.asarray(lengths, jnp.int32))

    lengths = jnp.where(number % 4 == 0, named(crowded, number // 4), named(common, number - number // 4 - 1))
    mixed = jax.random.permutation(jax.random.fold_in(own, 3), amount)
    source_of, receiver = mixed[0:amount // 2 * 2:2], mixed[1:amount // 2 * 2:2]
    room = jnp.minimum(lengths[source_of] - 1, most - lengths[receiver]) // 2
    room = jnp.where((source_of == sequence[0]) | (receiver == sequence[0]) | (lengths[receiver] == 0), 0, jnp.maximum(room, 0))
    passed = jax.random.randint(jax.random.fold_in(own, 4), (amount // 2,), 0, 1 << 20) % (room + 1)
    lengths = lengths.at[source_of].add(-passed).at[receiver].add(passed)
    items = jnp.searchsorted(jnp.cumsum(lengths), jnp.arange(rows * top), side="right").astype(jnp.int32)
    table = items.reshape(top, rows).T
    table = table[jax.random.permutation(jax.random.fold_in(own, 1), rows)]
    turn = jax.random.randint(jax.random.fold_in(own, 2), (rows, 1), 0, top)
    return jnp.take_along_axis(table, (jnp.arange(top)[None, :] + turn) % top, axis=1)


def portions_of(amount, total, most, skew, full):
    loads = [(1 << 20) // math.isqrt(grade ** skew) + 1 for grade in range(1, amount + 1)]
    largest = most if full else min(most, max(-(-total // amount), total * loads[0] // sum(loads)))
    least = 1 if total - largest >= amount - 1 else 0
    given, rest = [largest] + [least] * (amount - 1), total - largest - least * (amount - 1)
    while rest > 0:
        candidates = [i for i in range(1, amount) if given[i] < largest] or [i for i in range(1, amount) if given[i] < most]
        pool, budget = sum([loads[i] for i in candidates]), rest
        for i in candidates:
            addition = min(most - given[i], max(1, budget * loads[i] // pool), rest)
            given[i] = given[i] + addition
            rest = rest - addition
    return np.array(given)


def scatter_about(stream_key, dims, deviation, bound, cuts=(), held_as=jnp.bfloat16):
    factor_of = shard_levels(stream_key, dims, cuts, -0.22, 0.18) if cuts else 1.0
    drawn = jax.random.normal(stream_key, dims, jnp.float32) * deviation * factor_of
    return jnp.minimum(jnp.maximum(drawn, -bound), bound).astype(held_as)


def setup_inputs(seed: int = 0) -> dict:
    splits = jax.random.split(jax.random.key(seed), 13)
    query = draw_query(jax.random.fold_in(splits[12], 71), 0)
    key_value = draw_key_value(jax.random.fold_in(splits[12], 71), 0)
    positions = draw_positions(jax.random.fold_in(splits[12], 71), 0)
    resid = scatter_about(splits[3], (SEQS, LENGTH, D), 1.0, 6.0, ((0, 8), (1, 4)))
    sinks = jnp.clip(jax.random.uniform(splits[4], (QH,), jnp.float32, -2.0, 3.0), -2.0, 3.0)
    o_weight = scatter_about(splits[5], (QH * HD, D), (QH * HD) ** -0.5, 0.125, ((0, 8),))
    norm_gain = jnp.clip(1.0 + 0.15 * jax.random.normal(splits[6], (D,), jnp.float32), 0.25, 1.75)
    expert_ids_keys = jax.random.split(jax.random.fold_in(splits[7], 1), SEQS * LENGTH // TOK_DEV)
    expert_ids_turns = jax.random.permutation(jax.random.fold_in(splits[7], 3), SEQS * LENGTH // TOK_DEV)
    expert_ids = jax.vmap(lambda own, number: deal_out(jax.random.fold_in(splits[7], 2), own, number, TOK_DEV, EXPERTS, TOP, CAP, 2))(expert_ids_keys, expert_ids_turns).reshape((SEQS, LENGTH, TOP))
    route_weights = jnp.clip(0.1 + 0.4 * jax.random.uniform(splits[8], (SEQS, LENGTH, TOP), jnp.float32) ** shard_levels(splits[8], (SEQS, LENGTH, TOP), ((0, 8), (1, 4)), -0.2, 0.2), 0.1, 0.5)
    w_gate = scatter_about(splits[9], (D, EXPERTS * FF_E), D ** -0.5, 0.15625, ((1, 32),))
    w_up = scatter_about(splits[10], (D, EXPERTS * FF_E), D ** -0.5, 0.15625, ((1, 32),))
    w_down = scatter_about(splits[11], (EXPERTS * FF_E, D), FF_E ** -0.5, 0.15625, ((0, 32),))
    return {"query": query, "key_value": key_value, "positions": positions, "resid": resid, "sinks": sinks, "o_weight": o_weight, "norm_gain": norm_gain, "expert_ids": expert_ids, "route_weights": route_weights, "w_gate": w_gate, "w_up": w_up, "w_down": w_down}


NEG_FILL = -1e+30

def sequence_attention(query, key_value, positions, sinks):
    length = query.shape[0]
    group = QH // KVH
    grouped = query.reshape(length, KVH, group, HD).astype(jnp.float32)
    keys = key_value[:, 0].reshape(length, KVH, HD).astype(jnp.float32)
    values = key_value[:, 1].reshape(length, KVH, HD).astype(jnp.float32)
    scores = jnp.einsum('qgjd,kgd->gjqk', grouped, keys, precision=lax.Precision.HIGHEST) * (1.0 / math.sqrt(HD))
    allowed = positions[None, :] <= positions[:, None]
    scores = jnp.where(allowed[None, None], scores, NEG_FILL)
    sink = sinks.reshape(KVH, group)[:, :, None]
    top = jnp.maximum(lax.optimization_barrier(jnp.max(scores, axis=-1)), sink)
    weights = jnp.exp(scores - top[..., None])
    total = lax.optimization_barrier(jnp.sum(weights, axis=-1)) + jnp.exp(sink - top)
    mixed = jnp.einsum('gjqk,kgd->gjqd', weights, values, precision=lax.Precision.HIGHEST) / total[..., None]
    mixed = jnp.transpose(mixed, (2, 0, 1, 3))
    return mixed.reshape(length, QH * HD).astype(jnp.bfloat16)

def reference(query, key_value, positions, resid, sinks, o_weight, norm_gain, expert_ids, route_weights, w_gate, w_up, w_down):
    attended = lax.map(lambda items: sequence_attention(items[0], items[1], items[2], sinks), (query, key_value, positions))
    tokens = SEQS * LENGTH
    attended = attended.reshape(tokens, QH * HD)
    mixed = resid.reshape(tokens, D).astype(jnp.float32) + jnp.dot(attended, o_weight, preferred_element_type=jnp.float32)
    normed = (mixed * lax.rsqrt(lax.optimization_barrier(jnp.mean(mixed * mixed, axis=-1, keepdims=True)) + 1e-05) * norm_gain).astype(jnp.bfloat16)
    n_choices = tokens * TOP
    most_rows = N_CTX * N_EXP * CAP
    flat_ids = expert_ids.reshape(n_choices).astype(jnp.int32)
    order = jnp.argsort(flat_ids, stable=True).astype(jnp.int32)
    counts = jnp.bincount(flat_ids, length=EXPERTS).astype(jnp.int32)
    starts = (jnp.cumsum(counts) - counts).astype(jnp.int32)
    sorted_rows = normed[order // TOP]
    padded = jnp.concatenate([sorted_rows, jnp.zeros((most_rows, D), jnp.bfloat16)], axis=0)
    width = FF_E // SLICES

    def one_expert(carry, expert):
        start = starts[expert]
        block = lax.dynamic_slice_in_dim(padded, start, most_rows, 0)
        gate = jnp.dot(block, lax.dynamic_slice_in_dim(w_gate, expert * FF_E, FF_E, 1), preferred_element_type=jnp.float32)
        lifted = jnp.dot(block, lax.dynamic_slice_in_dim(w_up, expert * FF_E, FF_E, 1), preferred_element_type=jnp.float32)
        active = (gate * jax.nn.sigmoid(1.702 * gate) * (lifted + 1.0)).astype(jnp.bfloat16)
        down = lax.dynamic_slice_in_dim(w_down, expert * FF_E, FF_E, 0)
        partials = jnp.einsum('msf,sfd->smd', active.reshape(most_rows, SLICES, width).astype(jnp.float32), down.reshape(SLICES, width, D).astype(jnp.float32), precision=lax.Precision.HIGHEST).astype(jnp.bfloat16)
        result = lax.optimization_barrier(jnp.sum(partials.astype(jnp.float32), axis=0)).astype(jnp.bfloat16)
        valid = jnp.arange(most_rows, dtype=jnp.int32) < counts[expert]
        result = jnp.where(valid[:, None], result, jnp.zeros((), jnp.bfloat16))
        current = lax.dynamic_slice_in_dim(carry, start, most_rows, 0)
        carry = lax.dynamic_update_slice_in_dim(carry, current + result, start, 0)
        return (carry, None)
    initial = jnp.zeros((n_choices + most_rows, D), jnp.bfloat16)
    collected, _ = lax.scan(one_expert, initial, jnp.arange(EXPERTS, dtype=jnp.int32))
    expert_out = jnp.zeros((n_choices, D), jnp.bfloat16).at[order].set(collected[:n_choices])
    expert_out = expert_out.reshape(tokens, TOP, D).astype(jnp.float32)
    final = mixed + lax.optimization_barrier(jnp.sum(route_weights.reshape(tokens, TOP, 1) * expert_out, axis=1))
    return final.astype(jnp.bfloat16).reshape(SEQS, LENGTH, D)
```

```python
import math

import jax
import jax.numpy as jnp
from jax import lax
from jax.sharding import PartitionSpec as P

D = 1440
QH = 32
KVH = 4
HD = 64
TOP = 4
SLICES = 4


NEG_FILL = -1e30


def passed_along(value, axis, by):
    length = lax.axis_size(axis)
    return lax.ppermute(value, axis, [(i, (i + by) % length) for i in range(length)])


def from_partner(block, axis, bit):
    count = lax.axis_size(axis)
    route = []
    for low in range(count):
        high = low | 1 << bit
        if high != low and high < count:
            route += [(low, high), (high, low)]
    return lax.ppermute(block, axis, route)


def attend(query, key_value, positions, sinks):
    rows = query.shape[0]
    group = QH // KVH
    width = KVH * HD
    coarse = (positions // 32).astype(jnp.bfloat16)[:, None]
    fine = (positions % 32).astype(jnp.bfloat16)[:, None]
    own = jnp.concatenate(
        [
            key_value.reshape(rows, 2 * width),
            coarse,
            fine,
            jnp.zeros((rows, 126), jnp.bfloat16),
        ],
        axis=1,
    )
    blocks = [own]
    for by in range(1, lax.axis_size("ctx")):
        blocks.append(passed_along(own, "ctx", by))
    whole = jnp.concatenate(blocks, axis=0)
    keys = whole[:, :width].reshape(-1, KVH, HD)
    values = whole[:, width : 2 * width].reshape(-1, KVH, HD)
    key_pos = whole[:, 2 * width].astype(jnp.int32) * 32 + whole[:, 2 * width + 1].astype(jnp.int32)
    grouped = query.reshape(rows, KVH, group, HD)
    scores = jnp.einsum("rgjd,sgd->gjrs", grouped, keys, preferred_element_type=jnp.float32) * (
        1.0 / math.sqrt(HD)
    )
    allowed = key_pos[None, :] <= positions[:, None]
    scores = jnp.where(allowed[None, None], scores, NEG_FILL)
    sink = sinks.reshape(KVH, group)[:, :, None]
    top = jnp.maximum(jnp.max(scores, axis=-1), sink)
    weights = jnp.exp(scores - top[..., None])
    total = jnp.sum(weights, axis=-1) + jnp.exp(sink - top)
    accum = jnp.einsum(
        "gjrs,sgd->gjrd",
        weights.astype(jnp.bfloat16),
        values,
        preferred_element_type=jnp.float32,
    )
    attended = accum / total[..., None]
    return jnp.transpose(attended, (2, 0, 1, 3)).reshape(rows, QH * HD).astype(jnp.bfloat16)


def whole_projection(o_weight):
    chips = lax.axis_size("exp") // 2
    same_core = [[2 * chip + core for chip in range(chips)] for core in range(2)]
    mine = lax.all_gather(o_weight, "exp", axis=0, axis_index_groups=same_core)
    other = from_partner(mine, "exp", 0)
    return mine, other


def feed_forward(block, w_gate, w_up, w_down):
    flat = block.reshape(-1, D)
    gate = jnp.dot(flat, w_gate, preferred_element_type=jnp.float32)
    lifted = jnp.dot(flat, w_up, preferred_element_type=jnp.float32)
    active = (gate * jax.nn.sigmoid(1.702 * gate) * (lifted + 1.0)).astype(jnp.bfloat16)
    return jnp.dot(active, w_down, preferred_element_type=jnp.float32)


def body(
    query,
    key_value,
    positions,
    resid,
    sinks,
    o_weight,
    norm_gain,
    expert_ids,
    route_weights,
    w_gate,
    w_up,
    w_down,
):
    rows = query.shape[1]
    mine, other = whole_projection(o_weight)
    attended = attend(query[0], key_value[0], positions[0], sinks)
    chips = lax.axis_size("exp") // 2
    halves = attended.reshape(rows, chips, 2, -1)
    core = lax.axis_index("exp") % 2
    even, odd = halves[:, :, 0].reshape(rows, -1), halves[:, :, 1].reshape(rows, -1)
    projected = jnp.dot(
        jnp.where(core == 0, even, odd), mine.reshape(-1, D), preferred_element_type=jnp.float32
    ) + jnp.dot(
        jnp.where(core == 0, odd, even), other.reshape(-1, D), preferred_element_type=jnp.float32
    )
    mixed = resid[0].astype(jnp.float32) + projected
    normed = (
        mixed * lax.rsqrt(jnp.mean(mixed * mixed, axis=-1, keepdims=True) + 1e-05) * norm_gain
    ).astype(jnp.bfloat16)
    n_ctx = lax.axis_size("ctx")
    n_exp = lax.axis_size("exp")
    n_experts = n_ctx * n_exp // SLICES
    per_row = n_exp // SLICES
    cap = max(2, rows * TOP // n_experts)
    n_slots = n_experts * cap
    chosen = expert_ids[0].reshape(rows * TOP)
    onehot = chosen[:, None] == jnp.arange(n_experts, dtype=jnp.int32)[None, :]
    order = jnp.arange(rows * TOP, dtype=jnp.int32)
    earlier = (order[None, :] < order[:, None]).astype(jnp.bfloat16)
    before = jnp.dot(earlier, onehot.astype(jnp.bfloat16), preferred_element_type=jnp.float32)
    rank = jnp.sum(jnp.where(onehot, before, 0.0), axis=1).astype(jnp.int32)
    slot = (chosen % per_row * n_ctx + chosen // per_row) * cap + rank
    placed = slot.reshape(rows, TOP)[:, :, None] == jnp.arange(n_slots, dtype=jnp.int32)
    taken = jnp.any(placed, axis=1).astype(jnp.bfloat16)
    combine = jnp.sum(jnp.where(placed, route_weights[0][:, :, None], 0.0), axis=1)
    outgoing = (
        lax.dot_general(
            taken, normed, (((0,), (0,)), ((), ())), preferred_element_type=jnp.float32
        )
        .astype(jnp.bfloat16)
        .reshape(per_row, n_ctx, cap, D)
    )
    arrived = lax.all_to_all(outgoing, "ctx", split_axis=1, concat_axis=1, tiled=True)
    pieces = arrived.reshape(n_exp, n_ctx // SLICES, cap, D)
    held = lax.all_to_all(pieces, "exp", split_axis=0, concat_axis=0, tiled=True)
    ffn = lambda block: feed_forward(block, w_gate, w_up, w_down)
    near = held.reshape(-1, D)
    near_core = from_partner(near, "exp", 0)
    far = from_partner(near, "exp", 1)
    far_core = from_partner(far, "exp", 0)
    out_near = ffn(near)
    back_near = from_partner(ffn(near_core).astype(jnp.bfloat16), "exp", 0)
    back_far = from_partner(ffn(far_core).astype(jnp.bfloat16), "exp", 0)
    sum_far = (ffn(far) + back_far.astype(jnp.float32)).astype(jnp.bfloat16)
    returned_far = from_partner(sum_far, "exp", 1)
    result = out_near + back_near.astype(jnp.float32) + returned_far.astype(jnp.float32)
    back = lax.all_to_all(
        result.astype(jnp.bfloat16).reshape(held.shape),
        "exp",
        split_axis=0,
        concat_axis=0,
        tiled=True,
    )
    returned = lax.all_to_all(
        back.reshape(per_row, n_ctx, cap, D), "ctx", split_axis=1, concat_axis=1, tiled=True
    )
    gathered = jnp.dot(
        combine,
        returned.reshape(n_slots, D).astype(jnp.float32),
        precision=lax.Precision.HIGHEST,
    )
    final = mixed + gathered
    return final.astype(jnp.bfloat16)[None]


def solution(mesh):
    return jax.shard_map(
        body,
        mesh=mesh,
        in_specs=(
            P("exp", "ctx", None),
            P("exp", "ctx", None, None),
            P("exp", "ctx"),
            P("exp", "ctx", None),
            P(),
            P("exp", None),
            P(),
            P("exp", "ctx", None),
            P("exp", "ctx", None),
            P(None, ("ctx", "exp")),
            P(None, ("ctx", "exp")),
            P(("ctx", "exp"), None),
        ),
        out_specs=P("exp", "ctx", None),
        check_vma=False,
    )
```

```python
import math

import jax
import jax.numpy as jnp
from jax import lax
from jax.sharding import PartitionSpec as P

D = 1440
QH = 32
KVH = 4
HD = 64
TOP = 4
SLICES = 4


NEG_FILL = -1e30


def passed_along(value, axis, by):
    length = lax.axis_size(axis)
    return lax.ppermute(value, axis, [(i, (i + by) % length) for i in range(length)])


def from_partner(block, axis, bit):
    count = lax.axis_size(axis)
    route = []
    for low in range(count):
        high = low | 1 << bit
        if high != low and high < count:
            route += [(low, high), (high, low)]
    return lax.ppermute(block, axis, route)


def attend(query, key_value, positions, sinks):
    rows = query.shape[0]
    group = QH // KVH
    width = KVH * HD
    coarse = (positions // 32).astype(jnp.bfloat16)[:, None]
    fine = (positions % 32).astype(jnp.bfloat16)[:, None]
    own = jnp.concatenate(
        [
            key_value.reshape(rows, 2 * width),
            coarse,
            fine,
            jnp.zeros((rows, 126), jnp.bfloat16),
        ],
        axis=1,
    )
    blocks = [own]
    for by in range(1, lax.axis_size("ctx")):
        blocks.append(passed_along(own, "ctx", by))
    whole = jnp.concatenate(blocks, axis=0)
    keys = whole[:, :width].reshape(-1, KVH, HD)
    values = whole[:, width : 2 * width].reshape(-1, KVH, HD)
    key_pos = whole[:, 2 * width].astype(jnp.int32) * 32 + whole[:, 2 * width + 1].astype(jnp.int32)
    grouped = query.reshape(rows, KVH, group, HD)
    scores = jnp.einsum("rgjd,sgd->gjrs", grouped, keys, preferred_element_type=jnp.float32) * (
        1.0 / math.sqrt(HD)
    )
    allowed = key_pos[None, :] <= positions[:, None]
    scores = jnp.where(allowed[None, None], scores, NEG_FILL)
    sink = sinks.reshape(KVH, group)[:, :, None]
    top = jnp.maximum(jnp.max(scores, axis=-1), sink)
    weights = jnp.exp(scores - top[..., None])
    total = jnp.sum(weights, axis=-1) + jnp.exp(sink - top)
    accum = jnp.einsum(
        "gjrs,sgd->gjrd",
        weights.astype(jnp.bfloat16),
        values,
        preferred_element_type=jnp.float32,
    )
    attended = accum / total[..., None]
    return jnp.transpose(attended, (2, 0, 1, 3)).reshape(rows, QH * HD).astype(jnp.bfloat16)


def to_next_chip(block, by):
    count = lax.axis_size("exp")
    route = [(i, i + 2 * by) for i in range(count) if 0 <= i + 2 * by < count]
    return lax.ppermute(block, "exp", route)


def projection_blocks(o_weight):
    chips = lax.axis_size("exp") // 2
    chip = lax.axis_index("exp") // 2
    upward, downward = [o_weight], [o_weight]
    for _ in range(1, chips):
        upward.append(to_next_chip(upward[-1], 1))
        downward.append(to_next_chip(downward[-1], -1))
    blocks = [o_weight]
    for back in range(1, chips):
        blocks.append(jnp.where(back <= chip, upward[back], downward[chips - back]))
    return blocks, [from_partner(block, "exp", 0) for block in blocks]


def feed_forward(block, w_gate, w_up, w_down):
    flat = block.reshape(-1, D)
    gate = jnp.dot(flat, w_gate, preferred_element_type=jnp.float32)
    lifted = jnp.dot(flat, w_up, preferred_element_type=jnp.float32)
    active = (gate * jax.nn.sigmoid(1.702 * gate) * (lifted + 1.0)).astype(jnp.bfloat16)
    return jnp.dot(active, w_down, preferred_element_type=jnp.float32)


def body(
    query,
    key_value,
    positions,
    resid,
    sinks,
    o_weight,
    norm_gain,
    expert_ids,
    route_weights,
    w_gate,
    w_up,
    w_down,
):
    rows = query.shape[1]
    blocks, partner_blocks = projection_blocks(o_weight)
    attended = attend(query[0], key_value[0], positions[0], sinks)
    chips = lax.axis_size("exp") // 2
    halves = attended.reshape(rows, chips, 2, -1)
    chip, core = lax.axis_index("exp") // 2, lax.axis_index("exp") % 2
    even, odd = halves[:, :, 0], halves[:, :, 1]
    here, there = jnp.where(core == 0, even, odd), jnp.where(core == 0, odd, even)
    projected = jnp.zeros((rows, D), jnp.float32)
    for back in range(chips):
        source = (chip - back + chips) % chips
        for side, block in ((here, blocks[back]), (there, partner_blocks[back])):
            columns = lax.dynamic_index_in_dim(side, source, 1, keepdims=False)
            projected += jnp.dot(columns, block, preferred_element_type=jnp.float32)
    mixed = resid[0].astype(jnp.float32) + projected
    normed = (
        mixed * lax.rsqrt(jnp.mean(mixed * mixed, axis=-1, keepdims=True) + 1e-05) * norm_gain
    ).astype(jnp.bfloat16)
    n_ctx = lax.axis_size("ctx")
    n_exp = lax.axis_size("exp")
    n_experts = n_ctx * n_exp // SLICES
    per_row = n_exp // SLICES
    cap = max(2, rows * TOP // n_experts)
    n_slots = n_experts * cap
    chosen = expert_ids[0].reshape(rows * TOP)
    onehot = chosen[:, None] == jnp.arange(n_experts, dtype=jnp.int32)[None, :]
    order = jnp.arange(rows * TOP, dtype=jnp.int32)
    earlier = (order[None, :] < order[:, None]).astype(jnp.bfloat16)
    before = jnp.dot(earlier, onehot.astype(jnp.bfloat16), preferred_element_type=jnp.float32)
    rank = jnp.sum(jnp.where(onehot, before, 0.0), axis=1).astype(jnp.int32)
    slot = (chosen % per_row * n_ctx + chosen // per_row) * cap + rank
    placed = slot.reshape(rows, TOP)[:, :, None] == jnp.arange(n_slots, dtype=jnp.int32)
    taken = jnp.any(placed, axis=1).astype(jnp.bfloat16)
    combine = jnp.sum(jnp.where(placed, route_weights[0][:, :, None], 0.0), axis=1)
    outgoing = (
        lax.dot_general(
            taken, normed, (((0,), (0,)), ((), ())), preferred_element_type=jnp.float32
        )
        .astype(jnp.bfloat16)
        .reshape(per_row, n_ctx, cap, D)
    )
    arrived = lax.all_to_all(outgoing, "ctx", split_axis=1, concat_axis=1, tiled=True)
    pieces = arrived.reshape(n_exp, n_ctx // SLICES, cap, D)
    held = lax.all_to_all(pieces, "exp", split_axis=0, concat_axis=0, tiled=True)
    ffn = lambda block: feed_forward(block, w_gate, w_up, w_down)
    near = held.reshape(-1, D)
    near_core = from_partner(near, "exp", 0)
    far = from_partner(near, "exp", 1)
    far_core = from_partner(far, "exp", 0)
    out_near = ffn(near)
    back_near = from_partner(ffn(near_core).astype(jnp.bfloat16), "exp", 0)
    back_far = from_partner(ffn(far_core).astype(jnp.bfloat16), "exp", 0)
    sum_far = (ffn(far) + back_far.astype(jnp.float32)).astype(jnp.bfloat16)
    returned_far = from_partner(sum_far, "exp", 1)
    result = out_near + back_near.astype(jnp.float32) + returned_far.astype(jnp.float32)
    back = lax.all_to_all(
        result.astype(jnp.bfloat16).reshape(held.shape),
        "exp",
        split_axis=0,
        concat_axis=0,
        tiled=True,
    )
    returned = lax.all_to_all(
        back.reshape(per_row, n_ctx, cap, D), "ctx", split_axis=1, concat_axis=1, tiled=True
    )
    gathered = jnp.dot(
        combine,
        returned.reshape(n_slots, D).astype(jnp.float32),
        precision=lax.Precision.HIGHEST,
    )
    final = mixed + gathered
    return final.astype(jnp.bfloat16)[None]


def solution(mesh):
    return jax.shard_map(
        body,
        mesh=mesh,
        in_specs=(
            P("exp", "ctx", None),
            P("exp", "ctx", None, None),
            P("exp", "ctx"),
            P("exp", "ctx", None),
            P(),
            P("exp", None),
            P(),
            P("exp", "ctx", None),
            P("exp", "ctx", None),
            P(None, ("ctx", "exp")),
            P(None, ("ctx", "exp")),
            P(("ctx", "exp"), None),
        ),
        out_specs=P("exp", "ctx", None),
        check_vma=False,
    )
```

```python
import math

import jax
import jax.numpy as jnp
from jax import lax
from jax.sharding import PartitionSpec as P

D = 1440
QH = 32
KVH = 4
HD = 64
TOP = 4
SLICES = 4


NEG_FILL = -1e30


def passed_along(value, axis, by):
    length = lax.axis_size(axis)
    return lax.ppermute(value, axis, [(i, (i + by) % length) for i in range(length)])


def from_partner(block, axis, bit):
    count = lax.axis_size(axis)
    route = []
    for low in range(count):
        high = low | 1 << bit
        if high != low and high < count:
            route += [(low, high), (high, low)]
    return lax.ppermute(block, axis, route)


def attend(query, key_value, positions, sinks):
    rows = query.shape[0]
    group = QH // KVH
    width = KVH * HD
    coarse = (positions // 32).astype(jnp.bfloat16)[:, None]
    fine = (positions % 32).astype(jnp.bfloat16)[:, None]
    own = jnp.concatenate(
        [
            key_value.reshape(rows, 2 * width),
            coarse,
            fine,
            jnp.zeros((rows, 126), jnp.bfloat16),
        ],
        axis=1,
    )
    blocks = [own]
    for by in range(1, lax.axis_size("ctx")):
        blocks.append(passed_along(own, "ctx", by))
    whole = jnp.concatenate(blocks, axis=0)
    keys = whole[:, :width].reshape(-1, KVH, HD)
    values = whole[:, width : 2 * width].reshape(-1, KVH, HD)
    key_pos = whole[:, 2 * width].astype(jnp.int32) * 32 + whole[:, 2 * width + 1].astype(jnp.int32)
    grouped = query.reshape(rows, KVH, group, HD)
    scores = jnp.einsum("rgjd,sgd->gjrs", grouped, keys, preferred_element_type=jnp.float32) * (
        1.0 / math.sqrt(HD)
    )
    allowed = key_pos[None, :] <= positions[:, None]
    scores = jnp.where(allowed[None, None], scores, NEG_FILL)
    sink = sinks.reshape(KVH, group)[:, :, None]
    top = jnp.maximum(jnp.max(scores, axis=-1), sink)
    weights = jnp.exp(scores - top[..., None])
    total = jnp.sum(weights, axis=-1) + jnp.exp(sink - top)
    accum = jnp.einsum(
        "gjrs,sgd->gjrd",
        weights.astype(jnp.bfloat16),
        values,
        preferred_element_type=jnp.float32,
    )
    attended = accum / total[..., None]
    return jnp.transpose(attended, (2, 0, 1, 3)).reshape(rows, QH * HD).astype(jnp.bfloat16)


def to_next_chip(block, by):
    count = lax.axis_size("exp")
    route = [(i, i + 2 * by) for i in range(count) if 0 <= i + 2 * by < count]
    return lax.ppermute(block, "exp", route)


def projection_blocks(o_weight):
    chips = lax.axis_size("exp") // 2
    chip = lax.axis_index("exp") // 2
    upward, downward = [o_weight], [o_weight]
    for _ in range(1, chips):
        upward.append(to_next_chip(upward[-1], 1))
        downward.append(to_next_chip(downward[-1], -1))
    blocks = [o_weight]
    for back in range(1, chips):
        blocks.append(jnp.where(back <= chip, upward[back], downward[chips - back]))
    return blocks, [from_partner(block, "exp", 0) for block in blocks]


def feed_forward(block, w_gate, w_up, w_down):
    flat = block.reshape(-1, D)
    gate = jnp.dot(flat, w_gate, preferred_element_type=jnp.float32)
    lifted = jnp.dot(flat, w_up, preferred_element_type=jnp.float32)
    active = (gate * jax.nn.sigmoid(1.702 * gate) * (lifted + 1.0)).astype(jnp.bfloat16)
    return jnp.dot(active, w_down, preferred_element_type=jnp.float32)


def body(
    query,
    key_value,
    positions,
    resid,
    sinks,
    o_weight,
    norm_gain,
    expert_ids,
    route_weights,
    w_gate,
    w_up,
    w_down,
):
    rows = query.shape[1]
    blocks, partner_blocks = projection_blocks(o_weight)
    attended = attend(query[0], key_value[0], positions[0], sinks)
    chips = lax.axis_size("exp") // 2
    halves = attended.reshape(rows, chips, 2, -1)
    chip, core = lax.axis_index("exp") // 2, lax.axis_index("exp") % 2
    even, odd = halves[:, :, 0], halves[:, :, 1]
    here, there = jnp.where(core == 0, even, odd), jnp.where(core == 0, odd, even)
    projected = jnp.zeros((rows, D), jnp.float32)
    for back in range(chips):
        source = (chip - back + chips) % chips
        for side, block in ((here, blocks[back]), (there, partner_blocks[back])):
            columns = lax.dynamic_index_in_dim(side, source, 1, keepdims=False)
            projected += jnp.dot(columns, block, preferred_element_type=jnp.float32)
    mixed = resid[0].astype(jnp.float32) + projected
    normed = (
        mixed * lax.rsqrt(jnp.mean(mixed * mixed, axis=-1, keepdims=True) + 1e-05) * norm_gain
    ).astype(jnp.bfloat16)
    n_ctx = lax.axis_size("ctx")
    n_exp = lax.axis_size("exp")
    n_experts = n_ctx * n_exp // SLICES
    per_row = n_exp // SLICES
    cap = max(2, rows * TOP // n_experts)
    n_slots = n_experts * cap
    chosen = expert_ids[0].reshape(rows * TOP)
    onehot = chosen[:, None] == jnp.arange(n_experts, dtype=jnp.int32)[None, :]
    order = jnp.arange(rows * TOP, dtype=jnp.int32)
    earlier = (order[None, :] < order[:, None]).astype(jnp.bfloat16)
    before = jnp.dot(earlier, onehot.astype(jnp.bfloat16), preferred_element_type=jnp.float32)
    rank = jnp.sum(jnp.where(onehot, before, 0.0), axis=1).astype(jnp.int32)
    slot = (chosen % per_row * n_ctx + chosen // per_row) * cap + rank
    placed = slot.reshape(rows, TOP)[:, :, None] == jnp.arange(n_slots, dtype=jnp.int32)
    taken = jnp.any(placed, axis=1).astype(jnp.bfloat16)
    combine = jnp.sum(jnp.where(placed, route_weights[0][:, :, None], 0.0), axis=1)
    outgoing = (
        lax.dot_general(
            taken, normed, (((0,), (0,)), ((), ())), preferred_element_type=jnp.float32
        )
        .astype(jnp.bfloat16)
        .reshape(per_row, n_ctx, cap, D)
    )
    arrived = lax.all_to_all(outgoing, "ctx", split_axis=1, concat_axis=1, tiled=True)
    pieces = arrived.reshape(n_exp, n_ctx // SLICES, cap, D)
    held = lax.all_to_all(pieces, "exp", split_axis=0, concat_axis=0, tiled=True)
    ffn = lambda block: feed_forward(block, w_gate, w_up, w_down)
    near = held.reshape(-1, D)
    near_core = from_partner(near, "exp", 0)
    far = from_partner(near, "exp", 1)
    out_near = ffn(near)
    out_near_core = ffn(near_core).astype(jnp.bfloat16)
    far, out_near, out_near_core = lax.optimization_barrier((far, out_near, out_near_core))
    far_core = from_partner(far, "exp", 0)
    back_near = from_partner(out_near_core, "exp", 0)
    back_far = from_partner(ffn(far_core).astype(jnp.bfloat16), "exp", 0)
    sum_far = (ffn(far) + back_far.astype(jnp.float32)).astype(jnp.bfloat16)
    returned_far = from_partner(sum_far, "exp", 1)
    result = out_near + back_near.astype(jnp.float32) + returned_far.astype(jnp.float32)
    back = lax.all_to_all(
        result.astype(jnp.bfloat16).reshape(held.shape),
        "exp",
        split_axis=0,
        concat_axis=0,
        tiled=True,
    )
    returned = lax.all_to_all(
        back.reshape(per_row, n_ctx, cap, D), "ctx", split_axis=1, concat_axis=1, tiled=True
    )
    gathered = jnp.dot(
        combine,
        returned.reshape(n_slots, D).astype(jnp.float32),
        precision=lax.Precision.HIGHEST,
    )
    final = mixed + gathered
    return final.astype(jnp.bfloat16)[None]


def solution(mesh):
    return jax.shard_map(
        body,
        mesh=mesh,
        in_specs=(
            P("exp", "ctx", None),
            P("exp", "ctx", None, None),
            P("exp", "ctx"),
            P("exp", "ctx", None),
            P(),
            P("exp", None),
            P(),
            P("exp", "ctx", None),
            P("exp", "ctx", None),
            P(None, ("ctx", "exp")),
            P(None, ("ctx", "exp")),
            P(("ctx", "exp"), None),
        ),
        out_specs=P("exp", "ctx", None),
        check_vma=False,
    )
```
